128 devices in a mesh: vocab: 32 (over x, y, core), rows: 4 (over z).
Axes of the slice: x: 4, y: 4, z: 4, core: 2. Of those that a mesh axis runs over, the one named last changes fastest.
Arguments:
- hidden_states: bfloat16 [2048, 5120], P('rows', 'vocab'), may hold values from -104 to 104
- head_weight: bfloat16 [5120, 151936], P(None, ('vocab', 'rows')), may hold values from -0.078125 to 0.078125
- sign_bits: int32 [151936], P(('vocab', 'rows')), may hold values from 0 to 1
- bucket_ids: int32 [151936], P(('vocab', 'rows')), may hold values from 0 to 511
Outputs:
- sketch: float32 [2048, 512], P('rows', 'vocab')
- peak_logprob: float32 [2048], P('rows')
The draws below stay inside these ranges and needn't reach their ends.
All inputs are finite; a program needn't handle non-finite values.
Results may differ from the reference program's by a relative error of at most 0.0025.
Values may be sent and summed in bfloat16 or wider, within the bound.
No kernel may reach another device: no remote copies, remote signals or barrier semaphores. Data moves between devices by JAX's collectives and lax.ppermute only.
A program may use at most 128 MiB of HBM per device.

```python
import math
import jax
import jax.numpy as jnp
from jax import lax

D = 5120
V = 151936
B = 512
TOKENS = 2048


def draw_hidden_states(key, part):
    key = jax.random.fold_in(key, 11)
    key_values = jax.random.fold_in(key, 1)
    key_scale = jax.random.fold_in(key, 2)
    row_scale = jnp.exp(jax.random.uniform(key_scale, (TOKENS, 1), jnp.float32, 0.0, math.log(10.0)))
    values = jax.random.truncated_normal(key_values, -4.0, 4.0, (TOKENS, D), jnp.float32)
    return (values * row_scale).astype(jnp.bfloat16)


def touch_ends(entries, own_key, low, largest):
    shape = entries.shape
    index_at = [jax.random.randint(jax.random.fold_in(own_key, axis), (), 0, shape[axis]) for axis in range(len(shape))]
    entries = entries.at[tuple(index_at)].set(low)
    longest = shape.index(max(shape))
    index_at[longest] = (index_at[longest] + 1) % shape[longest]
    return entries.at[tuple(index_at)].set(largest)


def shard_levels(rng, shape, split, smallest, top_value):
    factor_of, own = 1.0, jax.random.fold_in(rng, 6)
    for position, blocks in split:
        heights = jnp.exp(jax.random.uniform(jax.random.fold_in(own, position), (blocks,), jnp.float32, smallest / len(split), top_value / len(split)))
        factor_of = factor_of * jnp.repeat(heights, shape[position] // blocks).reshape([-1 if axis == position else 1 for axis in range(len(shape))])
    return factor_of


def gaussian(own_key, extent, deviation, bound, cuts=(), kind=jnp.bfloat16):
    values = jax.random.normal(own_key, extent, jnp.float32) * deviation
    if len(cuts) > 0:
        values = shard_levels(own_key, extent, cuts, -0.22, 0.18) * values
    return jnp.clip(values, min=-bound, max=bound).astype(kind)


def setup_inputs(seed: int = 0) -> dict:
    streams_of = jax.random.split(jax.random.key(seed), 5)
    hidden_states = draw_hidden_states(jax.random.fold_in(streams_of[4], 71), 0)
    head_weight = gaussian(streams_of[1], (D, V), D ** -0.5, 0.078125, ((1, 128),))
    sign_bits = touch_ends(jax.random.randint(streams_of[2], (V,), 0, 2), jax.random.fold_in(streams_of[2], 1), 0, 1).astype(jnp.int32)
    bucket_ids = touch_ends(jax.random.randint(streams_of[3], (V,), 0, B), jax.random.fold_in(streams_of[3], 1), 0, B - 1).astype(jnp.int32)
    return dict(hidden_states=hidden_states, head_weight=head_weight, sign_bits=sign_bits, bucket_ids=bucket_ids)


def reference(hidden_states, head_weight, sign_bits, bucket_ids):
    logits = jnp.dot(hidden_states, head_weight, preferred_element_type=jnp.float32)
    row_max = lax.optimization_barrier(jnp.max(logits, axis=1))
    exponent = jnp.exp(logits - row_max[:, None])
    row_total = lax.optimization_barrier(jnp.sum(exponent, axis=1))
    peak_logprob = -jnp.log(row_total)
    exponent_bf = exponent.astype(jnp.bfloat16).astype(jnp.float32)
    signs = (2 * sign_bits - 1).astype(jnp.float32)
    signed_mass = jnp.transpose(exponent_bf * signs[None, :])
    bucket_sums = jnp.transpose(jax.ops.segment_sum(signed_mass, bucket_ids, num_segments=B))
    factor = jnp.sqrt(jnp.float32(V) * jnp.float32(B))
    sketch = bucket_sums / row_total[:, None] * factor
    return (sketch, peak_logprob)
```

```python
import functools

import jax
import jax.numpy as jnp
from jax import lax
from jax.experimental import pallas as pl
from jax.experimental.pallas import tpu as pltpu
from jax.sharding import PartitionSpec as P

V = 151936
B = 512
LANES = 128


def split_bf16(value):
    high = value.astype(jnp.bfloat16).astype(jnp.float32)
    low = (value - high).astype(jnp.bfloat16).astype(jnp.float32)
    return high, low


def sketch_kernel(w_ref, x_ref, ids_ref, sign_ref, out_ref, table_ref, *, groups, owners):
    columns = w_ref.shape[0]
    own = B // owners

    @pl.when(pl.program_id(0) == 0)
    def _():
        buckets = lax.broadcasted_iota(jnp.int32, (B, columns), 0)
        signs = (2 * sign_ref[...] - 1).astype(jnp.float32)
        table_ref[...] = jnp.where(buckets == ids_ref[...], signs, 0.0).astype(jnp.bfloat16)

    logits = jnp.dot(w_ref[...], x_ref[0], preferred_element_type=jnp.float32)
    max_high, max_low = split_bf16(jnp.max(logits, axis=0, keepdims=True))
    exponent = jnp.exp(logits - (max_high + max_low))
    total_high, total_low = split_bf16(jnp.sum(exponent, axis=0, keepdims=True))
    sums = jnp.dot(table_ref[...], exponent.astype(jnp.bfloat16), preferred_element_type=jnp.float32)
    for g in range(groups):
        lanes = slice(LANES * g, LANES * g + LANES)
        out_ref[:, 0, own * g : own * g + own, :] = sums[:, lanes].reshape(owners, own, LANES)
    rows = [kind[:, LANES * g : LANES * g + LANES] for kind in (max_high, max_low, total_high, total_low) for g in range(groups)]
    stats = jnp.concatenate(rows, axis=0)
    out_ref[:, 0, own * groups :, :] = jnp.broadcast_to(stats[None], (owners,) + stats.shape)


def partial_sums(weights, tokens, bucket_ids, sign_bits, owners):
    columns, depth = weights.shape
    blocks, _, width = tokens.shape
    groups = width // LANES
    rows = (B // owners + 4) * groups
    return pl.pallas_call(
        functools.partial(sketch_kernel, groups=groups, owners=owners),
        grid=(blocks,),
        in_specs=[
            pl.BlockSpec((columns, depth), lambda i: (0, 0), pipeline_mode=pl.Buffered(1)),
            pl.BlockSpec((1, depth, width), lambda i: (i, 0, 0)),
            pl.BlockSpec((1, columns), lambda i: (0, 0)),
            pl.BlockSpec((1, columns), lambda i: (0, 0)),
        ],
        out_specs=pl.BlockSpec((owners, 1, rows, LANES), lambda i: (0, i, 0, 0)),
        out_shape=jax.ShapeDtypeStruct((owners, blocks, rows, LANES), jnp.float32),
        scratch_shapes=[pltpu.VMEM((B, columns), jnp.bfloat16)],
        compiler_params=pltpu.CompilerParams(vmem_limit_bytes=56 * 2**20),
        cost_estimate=pl.CostEstimate(
            flops=2 * columns * (depth + B) * blocks * width,
            bytes_accessed=2 * depth * (columns + blocks * width),
            transcendentals=columns * blocks * width,
        ),
    )(weights, tokens, bucket_ids[None, :], sign_bits[None, :])


def per_device(hidden_states, head_weight, sign_bits, bucket_ids):
    owners = lax.axis_size("vocab")
    blocks = lax.axis_size("rows")
    width = hidden_states.shape[0]
    groups = width // LANES
    own = B // owners
    tokens = lax.all_gather(hidden_states.T, ("rows", "vocab"), axis=0, tiled=True)
    tokens = tokens.reshape(blocks, owners * hidden_states.shape[1], width)
    parts = partial_sums(head_weight.T, tokens, bucket_ids, sign_bits, owners)
    sent = parts.astype(jnp.float16).reshape(owners * blocks, parts.shape[2], LANES)
    received = lax.all_to_all(sent, ("vocab", "rows"), 0, 0, tiled=True).astype(jnp.float32)
    sums = received[:, : own * groups].reshape(-1, groups, own, LANES)
    stats = received[:, own * groups :].reshape(-1, 4, groups, LANES)
    local_max = stats[:, 0] + stats[:, 1]
    row_max = jnp.max(local_max, axis=0)
    rescale = jnp.exp(local_max - row_max)
    row_total = jnp.sum((stats[:, 2] + stats[:, 3]) * rescale, axis=0)
    bucket_sums = jnp.sum(sums * rescale[:, :, None, :], axis=0)
    factor = jnp.sqrt(jnp.float32(V) * jnp.float32(B))
    sketch = bucket_sums / row_total[:, None, :] * factor
    return (sketch.transpose(0, 2, 1).reshape(width, own), -jnp.log(row_total).reshape(width))


def solution(mesh):
    return jax.shard_map(
        per_device,
        mesh=mesh,
        in_specs=(
            P("rows", "vocab"),
            P(None, ("vocab", "rows")),
            P(("vocab", "rows")),
            P(("vocab", "rows")),
        ),
        out_specs=(P("rows", "vocab"), P("rows")),
        check_vma=False,
    )
```

```python
import functools

import jax
import jax.numpy as jnp
from jax import lax
from jax.experimental import pallas as pl
from jax.experimental.pallas import tpu as pltpu
from jax.sharding import PartitionSpec as P

V = 151936
B = 512
LANES = 128
SIDE = 4
CORES = 2
PLANE = SIDE * SIDE
DEVICES = SIDE * PLANE * CORES
OWN = B // (PLANE * CORES)
KINDS = 4
BOTH = ("vocab", "rows")
X, Y, Z = 0, 1, 2
ROW_BLOCK = 304
VMEM_BYTES = 44 * 2**20
PLACE_BYTES = 32 * 2**20
ANY = pl.BlockSpec(memory_space=pl.ANY)


def coordinates(device):
    vocab, z = divmod(device, SIDE)
    chip, core = divmod(vocab, CORES)
    return chip // SIDE, chip % SIDE, z, core


def device_at(x, y, z, core):
    return ((x * SIDE + y) * CORES + core) * SIDE + z


def permute(array, target):
    pairs = [(i, device_at(*target(*coordinates(i)))) for i in range(DEVICES)]
    return lax.ppermute(array, BOTH, pairs)


def shift(array, axis, step):
    def target(x, y, z, core):
        place = [x, y, z]
        place[axis] = (place[axis] + step) % SIDE
        return (*place, core)

    return permute(array, target)


def ring(array, axis):
    def target(x, y, z, core):
        place = [x, y, z]
        place[axis] = (place[axis] + (1 if core == 0 else -1)) % SIDE
        return (*place, core)

    return permute(array, target)


def swap(array):
    return permute(array, lambda x, y, z, core: (x, y, z, 1 - core))


def position():
    vocab = lax.axis_index("vocab")
    chip = vocab // CORES
    return (chip // SIDE, chip % SIDE, lax.axis_index("rows")), vocab % CORES


def place_first_kernel(own, lower, upper, far, out_a, out_b, sem):
    coords, _ = position()
    half = out_a.shape[2]
    copies = []
    for k, (piece, step) in enumerate(((own, 0), (lower, -1), (upper, 1), (far, 2))):
        slot = lax.rem(coords[Y] + SIDE + step, SIDE)
        copies.append(pltpu.make_async_copy(piece.at[:, pl.ds(0, half)], out_a.at[slot], sem.at[2 * k]))
        copies.append(pltpu.make_async_copy(piece.at[:, pl.ds(half, half)], out_b.at[slot], sem.at[2 * k + 1]))
    for copy in copies:
        copy.start()
    for copy in copies:
        copy.wait()


def place_second_kernel(*refs):
    coords, _ = position()
    outs, sem = refs[8:10], refs[10]
    copies = []
    for part, axis in enumerate((X, Z)):
        for k, step in enumerate((0, -1, 1, 2)):
            slot = lax.rem(coords[axis] + SIDE + step, SIDE)
            copies.append(pltpu.make_async_copy(refs[4 * part + k], outs[part].at[slot], sem.at[4 * part + k]))
    for copy in copies:
        copy.start()
    for copy in copies:
        copy.wait()


def place(kernel, pieces, shape):
    return pl.pallas_call(
        kernel,
        out_shape=[jax.ShapeDtypeStruct(shape, pieces[0].dtype)] * 2,
        out_specs=[ANY] * 2,
        scratch_shapes=[pltpu.SemaphoreType.DMA((8,))],
        compiler_params=pltpu.CompilerParams(vmem_limit_bytes=PLACE_BYTES),
    )(*pieces)


def around(array, axis):
    return (array, shift(array, axis, 1), shift(array, axis, -1), shift(array, axis, 2))


def split_bf16(value):
    high = value.astype(jnp.bfloat16).astype(jnp.float32)
    low = (value - high).astype(jnp.bfloat16).astype(jnp.float32)
    return high, low


def summarise(logits, table, core, store):
    max_high, max_low = split_bf16(jnp.max(logits, axis=0, keepdims=True))
    exponent = jnp.exp(logits - (max_high + max_low))
    total_high, total_low = split_bf16(jnp.sum(exponent, axis=0, keepdims=True))
    sums = jnp.dot(table, exponent.astype(jnp.bfloat16), preferred_element_type=jnp.float32)
    groups = logits.shape[1] // LANES
    pieces = [sums[:, LANES * g : LANES * g + LANES].reshape(PLANE, CORES, OWN, LANES) for g in range(groups)]
    kinds = (max_high, max_low, total_high, total_low)
    stats = [[kind[:, LANES * g : LANES * g + LANES] for g in range(groups)] for kind in kinds]
    store(pieces, stats)


def write(piece_refs, pieces, stats, core):
    kept_ref, sent_ref = piece_refs
    for g, piece in enumerate(pieces):
        rows = slice(OWN * g, OWN * g + OWN)
        kept_ref[:, rows, :] = jnp.where(core == 0, piece[:, 0], piece[:, 1])
        sent_ref[:, rows, :] = jnp.where(core == 0, piece[:, 1], piece[:, 0])
    rows = jnp.concatenate([row for kind in stats for row in kind], axis=0)
    rows = jnp.broadcast_to(rows[None], (PLANE,) + rows.shape)
    kept_ref[:, OWN * len(pieces) :, :] = rows
    sent_ref[:, OWN * len(pieces) :, :] = rows


def whole_kernel(w_ref, table_ref, *refs, which):
    count = len(which)
    buffers, refs = refs[: 2 * count], refs[2 * count :]
    kept_out, sent_out, held, logits, kept, sent, sem = refs[-7:]
    step = pl.program_id(0)
    (_, _, z), core = position()
    columns, depth = table_ref.shape[1], w_ref.shape[1]
    half = held.shape[4] // count

    def loads():
        for b in range(count):
            lanes = pl.ds(half * b, half)
            for k in range(2):
                same = (which[b] != "back") == (k == 0)
                c = core if same else 1 - core
                yield pltpu.make_async_copy(buffers[2 * b + k], held.at[:, :, c, :, lanes], sem.at[2 * b + k])

    @pl.when(step == 0)
    def _():
        copies = list(loads())
        for copy in copies:
            copy.start()
        for copy in copies:
            copy.wait()

    tokens = held[...].reshape(depth, half * count)
    logits[pl.ds(pl.multiple_of(step * ROW_BLOCK, ROW_BLOCK), ROW_BLOCK), :] = jnp.dot(
        w_ref[...], tokens, preferred_element_type=jnp.float32
    )

    @pl.when(step == pl.num_programs(0) - 1)
    def _():
        direction = 2 * core - 1
        groups = half // LANES

        def store(pieces, stats):
            copies = []
            for b in range(count):
                part = slice(groups * b, groups * b + groups)
                write((kept.at[b], sent.at[b]), pieces[part], [kind[part] for kind in stats], core)
                move = {"own": 0, "near": direction, "back": -direction, "far": 2}[which[b]]
                block = lax.rem(z + SIDE + move, SIDE)
                copies.append(pltpu.make_async_copy(kept.at[b], kept_out.at[:, block], sem.at[2 * b]))
                copies.append(pltpu.make_async_copy(sent.at[b], sent_out.at[:, block], sem.at[2 * b + 1]))
            for copy in copies:
                copy.start()
            for copy in copies:
                copy.wait()

        summarise(logits[:columns, :], table_ref[...], core, store)


def message_rows(half):
    return (OWN + KINDS) * (half // LANES)


def whole_blocks(weights, table, which, buffers, previous):
    columns, depth = weights.shape
    features, half = buffers[0].shape[2:]
    count = len(which)
    width = half * count
    rows = message_rows(half)
    steps = pl.cdiv(columns, ROW_BLOCK)
    shape = jax.ShapeDtypeStruct((PLANE, SIDE, rows, LANES), jnp.float32)
    return pl.pallas_call(
        functools.partial(whole_kernel, which=which),
        grid=(steps,),
        in_specs=[pl.BlockSpec((ROW_BLOCK, depth), lambda i: (i, 0)), pl.BlockSpec(table.shape, lambda i: (0, 0))]
        + [ANY] * (2 * count + len(previous)),
        out_specs=[ANY, ANY],
        out_shape=[shape, shape],
        input_output_aliases={2 + 2 * count + k: k for k in range(len(previous))},
        scratch_shapes=[
            pltpu.VMEM((SIDE, SIDE, CORES, features, width), jnp.bfloat16),
            pltpu.VMEM((steps * ROW_BLOCK, width), jnp.float32),
            pltpu.VMEM((count, PLANE, rows, LANES), jnp.float32),
            pltpu.VMEM((count, PLANE, rows, LANES), jnp.float32),
            pltpu.SemaphoreType.DMA((2 * count,)),
        ],
        compiler_params=pltpu.CompilerParams(vmem_limit_bytes=VMEM_BYTES),
        cost_estimate=pl.CostEstimate(
            flops=2 * columns * (depth + B) * width,
            bytes_accessed=2 * depth * (columns + width),
            transcendentals=columns * width,
        ),
    )(weights, table, *buffers, *previous)


def finish_kernel(w_hbm, table_ref, *refs):
    far_a, part_b, refs = refs[:2], refs[2:10], refs[12:]
    outs_a, outs_b, refs = refs[:2], refs[2:4], refs[4:]
    weights, held, logits, kept, sent, w_sem, x_sem, out_sem = refs
    step = pl.program_id(0)
    (x, _, z), core = position()
    columns = table_ref.shape[1]
    half = held.shape[5] // 2
    groups = half // LANES
    depth = weights.shape[1]
    direction = 2 * core - 1

    def w_copy(k):
        rows = pl.ds(ROW_BLOCK * k, min(ROW_BLOCK, columns - ROW_BLOCK * k))
        return pltpu.make_async_copy(w_hbm.at[rows], weights.at[rows], w_sem.at[k])

    def fetch_b(pair, slot):
        for k in range(8):
            move = (0, 0, direction, direction, -direction, -direction, 2, 2)[k]
            c = core if k in (0, 2, 5, 6) else 1 - core
            for h in range(2):
                target = held.at[slot, lax.rem(x + SIDE + move, SIDE), :, c, :, pl.ds(half * h, half)]
                pltpu.make_async_copy(part_b[k].at[2 * pair + h], target, x_sem.at[slot]).start()

    def arrived(slot, lanes):
        target = held.at[slot, :, :, :, :, pl.ds(0, lanes)]
        pltpu.make_async_copy(target, target, x_sem.at[slot]).wait()

    def send(b, outs, block):
        for k, source in enumerate((kept, sent)):
            pltpu.make_async_copy(source.at[b], outs[k].at[:, block], out_sem.at[b, k]).start()

    @pl.when(step == 0)
    def _():
        for k in range(2):
            target = held.at[0, :, :, core if k == 0 else 1 - core, :, pl.ds(0, half)]
            pltpu.make_async_copy(far_a[k], target, x_sem.at[0]).start()
        for k in range(w_sem.shape[0]):
            w_copy(k).start()
        fetch_b(0, 1)
        arrived(0, half)
        tokens = held[0, :, :, :, :, :half].reshape(depth, half)
        for k in range(w_sem.shape[0]):
            w_copy(k).wait()
            rows = slice(ROW_BLOCK * k, min(columns, ROW_BLOCK * (k + 1)))
            logits[rows, :] = jnp.dot(weights[rows, :], tokens, preferred_element_type=jnp.float32)

        def store(pieces, stats):
            write((kept.at[0], sent.at[0]), pieces, stats, core)

        summarise(logits[...], table_ref[...], core, store)
        send(0, outs_a, lax.rem(z + 2, SIDE))

    @pl.when(step > 0)
    def _():
        slot = lax.rem(step, 2)

        @pl.when(step == 1)
        def _():
            fetch_b(1, 0)

        arrived(slot, 2 * half)
        tokens = held[slot].reshape(depth, 2 * half)
        product = jnp.dot(weights[...], tokens, preferred_element_type=jnp.float32)

        def store(pieces, stats):
            for h in range(2):
                part = slice(groups * h, groups * h + groups)
                b = 2 * step - 1 + h
                write((kept.at[b], sent.at[b]), pieces[part], [kind[part] for kind in stats], core)
                send(b, outs_b, 2 * step - 2 + h)

        summarise(product, table_ref[...], core, store)

    @pl.when(step == pl.num_programs(0) - 1)
    def _():
        for b in range(5):
            for k, source in enumerate((kept, sent)):
                pltpu.make_async_copy(source.at[b], source.at[b], out_sem.at[b, k]).wait()


def finish(weights, table, far_a, part_b, previous):
    columns, depth = weights.shape
    features, half = far_a[0].shape[2:]
    rows = message_rows(half)
    shape = jax.ShapeDtypeStruct((PLANE, SIDE, rows, LANES), jnp.float32)
    results = pl.pallas_call(
        finish_kernel,
        grid=(3,),
        in_specs=[ANY, pl.BlockSpec(table.shape, lambda i: (0, 0))] + [ANY] * 12,
        out_specs=[ANY] * 4,
        out_shape=[shape] * 4,
        input_output_aliases={12: 0, 13: 1},
        scratch_shapes=[
            pltpu.VMEM((columns, depth), jnp.bfloat16),
            pltpu.VMEM((2, SIDE, SIDE, CORES, features, 2 * half), jnp.bfloat16),
            pltpu.VMEM((columns, half), jnp.float32),
            pltpu.VMEM((5, PLANE, rows, LANES), jnp.float32),
            pltpu.VMEM((5, PLANE, rows, LANES), jnp.float32),
            pltpu.SemaphoreType.DMA((pl.cdiv(columns, ROW_BLOCK),)),
            pltpu.SemaphoreType.DMA((2,)),
            pltpu.SemaphoreType.DMA((5, 2)),
        ],
        compiler_params=pltpu.CompilerParams(vmem_limit_bytes=VMEM_BYTES),
        cost_estimate=pl.CostEstimate(
            flops=2 * columns * (depth + B) * 5 * half,
            bytes_accessed=2 * depth * (columns + 5 * half),
            transcendentals=columns * 5 * half,
        ),
    )(weights, table, *far_a, *part_b, *previous)
    return results[:2], results[2:]


def unpack(message, groups):
    lead = message.shape[:-2]
    sums = message[..., : OWN * groups, :].reshape(*lead, groups, OWN, LANES)
    stats = message[..., OWN * groups :, :].reshape(*lead, KINDS, groups, LANES)
    return sums, [stats[..., k, :, :] for k in range(KINDS)]


def merge(kept, received, groups):
    sums_a, (high_a, low_a, *total_a) = unpack(kept, groups)
    sums_b, (high_b, low_b, *total_b) = unpack(received, groups)
    larger = high_a + low_a >= high_b + low_b
    high = jnp.where(larger, high_a, high_b)
    low = jnp.where(larger, low_a, low_b)
    scale_a = jnp.exp(high_a + low_a - (high + low))
    scale_b = jnp.exp(high_b + low_b - (high + low))
    sums = sums_a * scale_a[..., None, :] + sums_b * scale_b[..., None, :]
    total = (total_a[0] + total_a[1]) * scale_a + (total_b[0] + total_b[1]) * scale_b
    total_high = lax.reduce_precision(total, 8, 7)
    lead = kept.shape[:-2]
    return [sums.reshape(*lead, OWN * groups, LANES), high, low, total_high, total - total_high]


def per_device(hidden_states, head_weight, sign_bits, bucket_ids):
    width, features = hidden_states.shape
    half = width // 2
    groups = half // LANES
    weights = head_weight.T
    columns = weights.shape[0]
    buckets = lax.broadcasted_iota(jnp.int32, (B, columns), 0)
    table = jnp.where(buckets == bucket_ids[None, :], 2 * sign_bits[None, :] - 1, 0).astype(jnp.bfloat16)

    part_a, part_b = place(place_first_kernel, around(hidden_states.T, Y), (SIDE, features, half))
    own = place(place_second_kernel, around(part_a, X) + around(part_b, Z), (SIDE, SIDE, features, half))
    near = [ring(p, a) for p, a in zip(own, (Z, X))]
    other = [swap(p) for p in own]
    message_a = whole_blocks(weights, table, ("own",), (own[0], other[0]), ())
    other, message_a = lax.optimization_barrier((other, message_a))
    near_other = [ring(p, a) for p, a in zip(other, (Z, X))]
    near = lax.optimization_barrier(near)
    near_other = lax.optimization_barrier(near_other)
    far = [ring(p, a) for p, a in zip(near, (Z, X))]
    back = [swap(p) for p in near]
    back_other = [swap(p) for p in near_other]
    message_a = whole_blocks(weights, table, ("near", "back"), (near[0], near_other[0], back[0], back_other[0]), message_a)
    far, back, back_other, message_a = lax.optimization_barrier((far, back, back_other, message_a))
    far_other = [swap(p) for p in far]
    part_b = (own[1], other[1], near[1], near_other[1], back[1], back_other[1], far[1], far_other[1])
    message_a, message_b = finish(weights, table, (far[0], far_other[0]), part_b, message_a)

    pieces = []
    for kept, sent in (message_a, message_b):
        pieces += merge(kept, swap(sent), groups)
    packed = jnp.concatenate(pieces, axis=2).astype(jnp.float16)
    teams = [[device_at(x, y, z, c) for x in range(SIDE) for y in range(SIDE) for z in range(SIDE)] for c in range(CORES)]
    packed = packed.reshape(PLANE * SIDE, packed.shape[2], LANES)
    received = lax.all_to_all(packed, BOTH, 0, 0, axis_index_groups=teams, tiled=True).astype(jnp.float32)
    sums, (high, low, *totals) = unpack(received.reshape(PLANE * SIDE, 2, -1, LANES), groups)
    local_max = high + low
    rescale = jnp.exp(local_max - jnp.max(local_max, axis=0))
    row_total = jnp.sum((totals[0] + totals[1]) * rescale, axis=0)
    bucket_sums = jnp.sum(sums * rescale[..., None, :], axis=0)
    factor = jnp.sqrt(jnp.float32(V) * jnp.float32(B))
    sketch = bucket_sums / row_total[..., None, :] * factor
    return (sketch.transpose(0, 1, 3, 2).reshape(width, OWN), -jnp.log(row_total).reshape(width))


def solution(mesh):
    return jax.shard_map(
        per_device,
        mesh=mesh,
        in_specs=(
            P("rows", "vocab"),
            P(None, ("vocab", "rows")),
            P(("vocab", "rows")),
            P(("vocab", "rows")),
        ),
        out_specs=(P("rows", "vocab"), P("rows")),
        check_vma=False,
    )
```

```python
import functools

import jax
import jax.numpy as jnp
from jax import lax
from jax.experimental import pallas as pl
from jax.experimental.pallas import tpu as pltpu
from jax.sharding import PartitionSpec as P

V = 151936
B = 512
LANES = 128
SIDE = 4
CORES = 2
PLANE = SIDE * SIDE
DEVICES = SIDE * PLANE * CORES
OWN = B // (PLANE * CORES)
KINDS = 4
BOTH = ("vocab", "rows")
X, Y, Z = 0, 1, 2
ROW_BLOCK = 304
VMEM_BYTES = 44 * 2**20
PLACE_BYTES = 32 * 2**20
ANY = pl.BlockSpec(memory_space=pl.ANY)


def coordinates(device):
    vocab, z = divmod(device, SIDE)
    chip, core = divmod(vocab, CORES)
    return chip // SIDE, chip % SIDE, z, core


def device_at(x, y, z, core):
    return ((x * SIDE + y) * CORES + core) * SIDE + z


def permute(array, target):
    pairs = [(i, device_at(*target(*coordinates(i)))) for i in range(DEVICES)]
    return lax.ppermute(array, BOTH, pairs)


def shift(array, axis, step):
    def target(x, y, z, core):
        place = [x, y, z]
        place[axis] = (place[axis] + step) % SIDE
        return (*place, core)

    return permute(array, target)


def ring(array, axis, sign=1):
    def target(x, y, z, core):
        place = [x, y, z]
        place[axis] = (place[axis] + (sign if core == 0 else -sign)) % SIDE
        return (*place, core)

    return permute(array, target)


def swap(array):
    return permute(array, lambda x, y, z, core: (x, y, z, 1 - core))


def position():
    vocab = lax.axis_index("vocab")
    chip = vocab // CORES
    return (chip // SIDE, chip % SIDE, lax.axis_index("rows")), vocab % CORES


def place_first_kernel(own, lower, upper, far, out_a, out_b, sem):
    coords, _ = position()
    half = out_a.shape[2]
    copies = []
    for k, (piece, step) in enumerate(((own, 0), (lower, -1), (upper, 1), (far, 2))):
        slot = lax.rem(coords[Y] + SIDE + step, SIDE)
        copies.append(pltpu.make_async_copy(piece.at[:, pl.ds(0, half)], out_a.at[slot], sem.at[2 * k]))
        copies.append(pltpu.make_async_copy(piece.at[:, pl.ds(half, half)], out_b.at[slot], sem.at[2 * k + 1]))
    for copy in copies:
        copy.start()
    for copy in copies:
        copy.wait()


def place_second_kernel(*refs):
    coords, core = position()
    outs, sem = refs[8:10], refs[10]
    copies = []
    for part, axis in enumerate((X, Z)):
        for k, step in enumerate((0, 2 * core - 1, 1 - 2 * core, 2)):
            slot = lax.rem(coords[axis] + SIDE + step, SIDE)
            copies.append(pltpu.make_async_copy(refs[4 * part + k], outs[part].at[slot], sem.at[4 * part + k]))
    for copy in copies:
        copy.start()
    for copy in copies:
        copy.wait()


def place(kernel, pieces, shape):
    return pl.pallas_call(
        kernel,
        out_shape=[jax.ShapeDtypeStruct(shape, pieces[0].dtype)] * 2,
        out_specs=[ANY] * 2,
        scratch_shapes=[pltpu.SemaphoreType.DMA((8,))],
        compiler_params=pltpu.CompilerParams(vmem_limit_bytes=PLACE_BYTES),
    )(*pieces)


def around(array, axis):
    return (array, shift(array, axis, 1), shift(array, axis, -1), shift(array, axis, 2))


def around_by_ring(array, axis):
    ahead = ring(array, axis)
    return (array, ahead, ring(array, axis, -1), ring(ahead, axis))


def summarise(logits, table, core, store):
    local_max = jnp.max(logits, axis=0, keepdims=True)
    exponent = jnp.exp(logits - local_max)
    total = jnp.sum(exponent, axis=0, keepdims=True)
    sums = jnp.dot(table, exponent.astype(jnp.bfloat16), preferred_element_type=jnp.float32)
    groups = logits.shape[1] // LANES
    pieces = [sums[:, LANES * g : LANES * g + LANES].reshape(PLANE, CORES, OWN, LANES) for g in range(groups)]
    kinds = (local_max, total, local_max, total)
    stats = [[kind[:, LANES * g : LANES * g + LANES] for g in range(groups)] for kind in kinds]
    store(pieces, stats)


def write(piece_refs, pieces, stats, core):
    kept_ref, sent_ref = piece_refs
    for g, piece in enumerate(pieces):
        rows = slice(OWN * g, OWN * g + OWN)
        kept_ref[:, rows, :] = jnp.where(core == 0, piece[:, 0], piece[:, 1])
        sent_ref[:, rows, :] = jnp.where(core == 0, piece[:, 1], piece[:, 0])
    rows = jnp.concatenate([row for kind in stats for row in kind], axis=0)
    rows = jnp.broadcast_to(rows[None], (PLANE,) + rows.shape)
    kept_ref[:, OWN * len(pieces) :, :] = rows
    sent_ref[:, OWN * len(pieces) :, :] = rows


def whole_kernel(w_ref, table_ref, *refs, which):
    count = len(which)
    buffers, refs = refs[: 2 * count], refs[2 * count :]
    kept_out, sent_out, held, logits, kept, sent, sem = refs[-7:]
    step = pl.program_id(0)
    (_, _, z), core = position()
    columns, depth = table_ref.shape[1], w_ref.shape[1]
    half = held.shape[4] // count

    def loads():
        for b in range(count):
            lanes = pl.ds(half * b, half)
            for k in range(2):
                same = (which[b] != "back") == (k == 0)
                c = core if same else 1 - core
                yield pltpu.make_async_copy(buffers[2 * b + k], held.at[:, :, c, :, lanes], sem.at[2 * b + k])

    @pl.when(step == 0)
    def _():
        copies = list(loads())
        for copy in copies:
            copy.start()
        for copy in copies:
            copy.wait()

    tokens = held[...].reshape(depth, half * count)
    logits[pl.ds(pl.multiple_of(step * ROW_BLOCK, ROW_BLOCK), ROW_BLOCK), :] = jnp.dot(
        w_ref[...], tokens, preferred_element_type=jnp.float32
    )

    @pl.when(step == pl.num_programs(0) - 1)
    def _():
        direction = 2 * core - 1
        groups = half // LANES

        def store(pieces, stats):
            copies = []
            for b in range(count):
                part = slice(groups * b, groups * b + groups)
                write((kept.at[b], sent.at[b]), pieces[part], [kind[part] for kind in stats], core)
                move = {"own": 0, "near": direction, "back": -direction, "far": 2}[which[b]]
                block = lax.rem(z + SIDE + move, SIDE)
                copies.append(pltpu.make_async_copy(kept.at[b], kept_out.at[:, block], sem.at[2 * b]))
                copies.append(pltpu.make_async_copy(sent.at[b], sent_out.at[:, block], sem.at[2 * b + 1]))
            for copy in copies:
                copy.start()
            for copy in copies:
                copy.wait()

        summarise(logits[:columns, :], table_ref[...], core, store)


def message_rows(half):
    return (OWN + KINDS) * (half // LANES)


def whole_blocks(weights, table, which, buffers, previous):
    columns, depth = weights.shape
    features, half = buffers[0].shape[2:]
    count = len(which)
    width = half * count
    rows = message_rows(half)
    steps = pl.cdiv(columns, ROW_BLOCK)
    shape = jax.ShapeDtypeStruct((PLANE, SIDE, rows, LANES), jnp.float32)
    return pl.pallas_call(
        functools.partial(whole_kernel, which=which),
        grid=(steps,),
        in_specs=[pl.BlockSpec((ROW_BLOCK, depth), lambda i: (i, 0)), pl.BlockSpec(table.shape, lambda i: (0, 0))]
        + [ANY] * (2 * count + len(previous)),
        out_specs=[ANY, ANY],
        out_shape=[shape, shape],
        input_output_aliases={2 + 2 * count + k: k for k in range(len(previous))},
        scratch_shapes=[
            pltpu.VMEM((SIDE, SIDE, CORES, features, width), jnp.bfloat16),
            pltpu.VMEM((steps * ROW_BLOCK, width), jnp.float32),
            pltpu.VMEM((count, PLANE, rows, LANES), jnp.float32),
            pltpu.VMEM((count, PLANE, rows, LANES), jnp.float32),
            pltpu.SemaphoreType.DMA((2 * count,)),
        ],
        compiler_params=pltpu.CompilerParams(vmem_limit_bytes=VMEM_BYTES),
        cost_estimate=pl.CostEstimate(
            flops=2 * columns * (depth + B) * width,
            bytes_accessed=2 * depth * (columns + width),
            transcendentals=columns * width,
        ),
    )(weights, table, *buffers, *previous)


def finish_kernel(w_hbm, table_ref, *refs):
    far_a, part_b, refs = refs[:2], refs[2:10], refs[12:]
    outs_a, outs_b, refs = refs[:2], refs[2:4], refs[4:]
    weights, held, logits, kept, sent, w_sem, x_sem, out_sem = refs
    step = pl.program_id(0)
    (x, _, z), core = position()
    columns = table_ref.shape[1]
    half = held.shape[5] // 2
    groups = half // LANES
    depth = weights.shape[1]
    direction = 2 * core - 1

    def w_copy(k):
        rows = pl.ds(ROW_BLOCK * k, min(ROW_BLOCK, columns - ROW_BLOCK * k))
        return pltpu.make_async_copy(w_hbm.at[rows], weights.at[rows], w_sem.at[k])

    def fetch_b(pair, slot):
        for k in range(8):
            move = (0, 0, direction, direction, -direction, -direction, 2, 2)[k]
            c = core if k in (0, 2, 5, 6) else 1 - core
            for h in range(2):
                target = held.at[slot, lax.rem(x + SIDE + move, SIDE), :, c, :, pl.ds(half * h, half)]
                pltpu.make_async_copy(part_b[k].at[2 * pair + h], target, x_sem.at[slot]).start()

    def arrived(slot, lanes):
        target = held.at[slot, :, :, :, :, pl.ds(0, lanes)]
        pltpu.make_async_copy(target, target, x_sem.at[slot]).wait()

    def send(b, outs, block):
        for k, source in enumerate((kept, sent)):
            pltpu.make_async_copy(source.at[b], outs[k].at[:, block], out_sem.at[b, k]).start()

    @pl.when(step == 0)
    def _():
        for k in range(2):
            target = held.at[0, :, :, core if k == 0 else 1 - core, :, pl.ds(0, half)]
            pltpu.make_async_copy(far_a[k], target, x_sem.at[0]).start()
        for k in range(w_sem.shape[0]):
            w_copy(k).start()
        fetch_b(0, 1)
        arrived(0, half)
        tokens = held[0, :, :, :, :, :half].reshape(depth, half)
        for k in range(w_sem.shape[0]):
            w_copy(k).wait()
            rows = slice(ROW_BLOCK * k, min(columns, ROW_BLOCK * (k + 1)))
            logits[rows, :] = jnp.dot(weights[rows, :], tokens, preferred_element_type=jnp.float32)

        def store(pieces, stats):
            write((kept.at[0], sent.at[0]), pieces, stats, core)

        summarise(logits[...], table_ref[...], core, store)
        send(0, outs_a, lax.rem(z + 2, SIDE))

    @pl.when(step > 0)
    def _():
        slot = lax.rem(step, 2)

        @pl.when(step == 1)
        def _():
            fetch_b(1, 0)

        arrived(slot, 2 * half)
        tokens = held[slot].reshape(depth, 2 * half)
        product = jnp.dot(weights[...], tokens, preferred_element_type=jnp.float32)

        def store(pieces, stats):
            for h in range(2):
                part = slice(groups * h, groups * h + groups)
                b = 2 * step - 1 + h
                write((kept.at[b], sent.at[b]), pieces[part], [kind[part] for kind in stats], core)
                send(b, outs_b, 2 * step - 2 + h)

        summarise(product, table_ref[...], core, store)

    @pl.when(step == pl.num_programs(0) - 1)
    def _():
        for b in range(5):
            for k, source in enumerate((kept, sent)):
                pltpu.make_async_copy(source.at[b], source.at[b], out_sem.at[b, k]).wait()


def finish(weights, table, far_a, part_b, previous):
    columns, depth = weights.shape
    features, half = far_a[0].shape[2:]
    rows = message_rows(half)
    shape = jax.ShapeDtypeStruct((PLANE, SIDE, rows, LANES), jnp.float32)
    results = pl.pallas_call(
        finish_kernel,
        grid=(3,),
        in_specs=[ANY, pl.BlockSpec(table.shape, lambda i: (0, 0))] + [ANY] * 12,
        out_specs=[ANY] * 4,
        out_shape=[shape] * 4,
        input_output_aliases={12: 0, 13: 1},
        scratch_shapes=[
            pltpu.VMEM((columns, depth), jnp.bfloat16),
            pltpu.VMEM((2, SIDE, SIDE, CORES, features, 2 * half), jnp.bfloat16),
            pltpu.VMEM((columns, half), jnp.float32),
            pltpu.VMEM((5, PLANE, rows, LANES), jnp.float32),
            pltpu.VMEM((5, PLANE, rows, LANES), jnp.float32),
            pltpu.SemaphoreType.DMA((pl.cdiv(columns, ROW_BLOCK),)),
            pltpu.SemaphoreType.DMA((2,)),
            pltpu.SemaphoreType.DMA((5, 2)),
        ],
        compiler_params=pltpu.CompilerParams(vmem_limit_bytes=VMEM_BYTES),
        cost_estimate=pl.CostEstimate(
            flops=2 * columns * (depth + B) * 5 * half,
            bytes_accessed=2 * depth * (columns + 5 * half),
            transcendentals=columns * 5 * half,
        ),
    )(weights, table, *far_a, *part_b, *previous)
    return results[:2], results[2:]


def unpack(message, groups):
    lead = message.shape[:-2]
    sums = message[..., : OWN * groups, :].reshape(*lead, groups, OWN, LANES)
    stats = message[..., OWN * groups :, :].reshape(*lead, KINDS, groups, LANES)
    return sums, [stats[..., k, :, :] for k in range(KINDS)]


def merge(kept, received, groups):
    sums_a, (max_a, total_a, *_) = unpack(kept, groups)
    sums_b, (max_b, total_b, *_) = unpack(received, groups)
    local_max = jnp.maximum(max_a, max_b)
    scale_a = jnp.exp(max_a - local_max)
    scale_b = jnp.exp(max_b - local_max)
    sums = sums_a * scale_a[..., None, :] + sums_b * scale_b[..., None, :]
    excess = total_a * scale_a + total_b * scale_b - 1.0
    high = lax.reduce_precision(local_max, 8, 7)
    middle = lax.reduce_precision(local_max - high, 8, 7)
    low = local_max - high - middle
    return [sums.reshape(*kept.shape[:-2], OWN * groups, LANES), high, middle, low, excess]


def per_device(hidden_states, head_weight, sign_bits, bucket_ids):
    width, features = hidden_states.shape
    half = width // 2
    groups = half // LANES
    weights = head_weight.T
    columns = weights.shape[0]
    buckets = lax.broadcasted_iota(jnp.int32, (B, columns), 0)
    table = jnp.where(buckets == bucket_ids[None, :], 2 * sign_bits[None, :] - 1, 0).astype(jnp.bfloat16)

    part_a, part_b = place(place_first_kernel, around(hidden_states.T, Y), (SIDE, features, half))
    own = place(place_second_kernel, around_by_ring(part_a, X) + around_by_ring(part_b, Z), (SIDE, SIDE, features, half))
    near = [ring(p, a) for p, a in zip(own, (Z, X))]
    other = [swap(p) for p in own]
    message_a = whole_blocks(weights, table, ("own",), (own[0], other[0]), ())
    other, message_a = lax.optimization_barrier((other, message_a))
    near_other = [ring(p, a) for p, a in zip(other, (Z, X))]
    near = lax.optimization_barrier(near)
    far = [ring(p, a) for p, a in zip(near, (Z, X))]
    back = [swap(p) for p in near]
    back_other = [swap(p) for p in near_other]
    message_a = whole_blocks(weights, table, ("near", "back"), (near[0], near_other[0], back[0], back_other[0]), message_a)
    far, back, back_other, message_a = lax.optimization_barrier((far, back, back_other, message_a))
    far_other = [swap(p) for p in far]
    part_b = (own[1], other[1], near[1], near_other[1], back[1], back_other[1], far[1], far_other[1])
    message_a, message_b = finish(weights, table, (far[0], far_other[0]), part_b, message_a)

    pieces = []
    for kept, sent in (message_a, message_b):
        pieces += merge(kept, swap(sent), groups)
    packed = jnp.concatenate(pieces, axis=2).astype(jnp.float16)
    teams = [[device_at(x, y, z, c) for x in range(SIDE) for y in range(SIDE) for z in range(SIDE)] for c in range(CORES)]
    packed = packed.reshape(PLANE * SIDE, packed.shape[2], LANES)
    received = lax.all_to_all(packed, BOTH, 0, 0, axis_index_groups=teams, tiled=True).astype(jnp.float32)
    sums, (high, middle, low, excess) = unpack(received.reshape(PLANE * SIDE, 2, -1, LANES), groups)
    local_max = high + middle + low
    rescale = jnp.exp(local_max - jnp.max(local_max, axis=0))
    row_total = jnp.sum((1.0 + excess) * rescale, axis=0)
    bucket_sums = jnp.sum(sums * rescale[..., None, :], axis=0)
    factor = jnp.sqrt(jnp.float32(V) * jnp.float32(B))
    sketch = bucket_sums / row_total[..., None, :] * factor
    return (sketch.transpose(0, 1, 3, 2).reshape(width, OWN), -jnp.log(row_total).reshape(width))


def solution(mesh):
    return jax.shard_map(
        per_device,
        mesh=mesh,
        in_specs=(
            P("rows", "vocab"),
            P(None, ("vocab", "rows")),
            P(("vocab", "rows")),
            P(("vocab", "rows")),
        ),
        out_specs=(P("rows", "vocab"), P("rows")),
        check_vma=False,
    )
```

```python
import functools

import jax
import jax.numpy as jnp
from jax import lax
from jax.experimental import pallas as pl
from jax.experimental.pallas import tpu as pltpu
from jax.sharding import PartitionSpec as P

V = 151936
B = 512
LANES = 128
SIDE = 4
CORES = 2
PLANE = SIDE * SIDE
DEVICES = SIDE * PLANE * CORES
OWN = B // (PLANE * CORES)
KINDS = 4
BOTH = ("vocab", "rows")
X, Y, Z = 0, 1, 2
ROW_BLOCK = 304
VMEM_BYTES = 44 * 2**20
PLACE_BYTES = 32 * 2**20
ANY = pl.BlockSpec(memory_space=pl.ANY)


def coordinates(device):
    vocab, z = divmod(device, SIDE)
    chip, core = divmod(vocab, CORES)
    return chip // SIDE, chip % SIDE, z, core


def device_at(x, y, z, core):
    return ((x * SIDE + y) * CORES + core) * SIDE + z


def permute(array, target):
    pairs = [(i, device_at(*target(*coordinates(i)))) for i in range(DEVICES)]
    return lax.ppermute(array, BOTH, pairs)


def shift(array, axis, step):
    def target(x, y, z, core):
        place = [x, y, z]
        place[axis] = (place[axis] + step) % SIDE
        return (*place, core)

    return permute(array, target)


def ring(array, axis, sign=1):
    def target(x, y, z, core):
        place = [x, y, z]
        place[axis] = (place[axis] + (sign if core == 0 else -sign)) % SIDE
        return (*place, core)

    return permute(array, target)


def swap(array):
    return permute(array, lambda x, y, z, core: (x, y, z, 1 - core))


def position():
    vocab = lax.axis_index("vocab")
    chip = vocab // CORES
    return (chip // SIDE, chip % SIDE, lax.axis_index("rows")), vocab % CORES


def place_first_kernel(own, lower, upper, far, out_a, out_b, sem):
    coords, _ = position()
    half = out_a.shape[2]
    copies = []
    for k, (piece, step) in enumerate(((own, 0), (lower, -1), (upper, 1), (far, 2))):
        slot = lax.rem(coords[Y] + SIDE + step, SIDE)
        copies.append(pltpu.make_async_copy(piece.at[:, pl.ds(0, half)], out_a.at[slot], sem.at[2 * k]))
        copies.append(pltpu.make_async_copy(piece.at[:, pl.ds(half, half)], out_b.at[slot], sem.at[2 * k + 1]))
    for copy in copies:
        copy.start()
    for copy in copies:
        copy.wait()


def place_second_kernel(*refs):
    coords, core = position()
    outs, sem = refs[8:10], refs[10]
    copies = []
    for part, axis in enumerate((X, Z)):
        for k, step in enumerate((0, 2 * core - 1, 1 - 2 * core, 2)):
            slot = lax.rem(coords[axis] + SIDE + step, SIDE)
            copies.append(pltpu.make_async_copy(refs[4 * part + k], outs[part].at[slot], sem.at[4 * part + k]))
    for copy in copies:
        copy.start()
    for copy in copies:
        copy.wait()


def place(kernel, pieces, shape):
    return pl.pallas_call(
        kernel,
        out_shape=[jax.ShapeDtypeStruct(shape, pieces[0].dtype)] * 2,
        out_specs=[ANY] * 2,
        scratch_shapes=[pltpu.SemaphoreType.DMA((8,))],
        compiler_params=pltpu.CompilerParams(vmem_limit_bytes=PLACE_BYTES),
    )(*pieces)


def around(array, axis):
    return (array, shift(array, axis, 1), shift(array, axis, -1), shift(array, axis, 2))


def around_by_ring(array, axis):
    ahead = ring(array, axis)
    return (array, ahead, ring(array, axis, -1), ring(ahead, axis))


def summarise(logits, table, core, store):
    local_max = jnp.max(logits, axis=0, keepdims=True)
    exponent = jnp.exp(logits - local_max)
    total = jnp.sum(exponent, axis=0, keepdims=True)
    sums = jnp.dot(table, exponent.astype(jnp.bfloat16), preferred_element_type=jnp.float32)
    groups = logits.shape[1] // LANES
    pieces = [sums[:, LANES * g : LANES * g + LANES].reshape(PLANE, CORES, OWN, LANES) for g in range(groups)]
    kinds = (local_max, total, local_max, total)
    stats = [[kind[:, LANES * g : LANES * g + LANES] for g in range(groups)] for kind in kinds]
    store(pieces, stats)


def write(piece_refs, pieces, stats, core):
    kept_ref, sent_ref = piece_refs
    for g, piece in enumerate(pieces):
        rows = slice(OWN * g, OWN * g + OWN)
        kept_ref[:, rows, :] = jnp.where(core == 0, piece[:, 0], piece[:, 1])
        sent_ref[:, rows, :] = jnp.where(core == 0, piece[:, 1], piece[:, 0])
    rows = jnp.concatenate([row for kind in stats for row in kind], axis=0)
    rows = jnp.broadcast_to(rows[None], (PLANE,) + rows.shape)
    kept_ref[:, OWN * len(pieces) :, :] = rows
    sent_ref[:, OWN * len(pieces) :, :] = rows


def whole_kernel(w_ref, table_ref, *refs, which):
    count = len(which)
    buffers, refs = refs[: 2 * count], refs[2 * count :]
    kept_out, sent_out, held, logits, kept, sent, sem = refs[-7:]
    step = pl.program_id(0)
    (_, _, z), core = position()
    columns, depth = table_ref.shape[1], w_ref.shape[1]
    half = held.shape[4] // count

    def loads():
        for b in range(count):
            lanes = pl.ds(half * b, half)
            for k in range(2):
                same = (which[b] != "back") == (k == 0)
                c = core if same else 1 - core
                yield pltpu.make_async_copy(buffers[2 * b + k], held.at[:, :, c, :, lanes], sem.at[2 * b + k])

    @pl.when(step == 0)
    def _():
        copies = list(loads())
        for copy in copies:
            copy.start()
        for copy in copies:
            copy.wait()

    tokens = held[...].reshape(depth, half * count)
    logits[pl.ds(pl.multiple_of(step * ROW_BLOCK, ROW_BLOCK), ROW_BLOCK), :] = jnp.dot(
        w_ref[...], tokens, preferred_element_type=jnp.float32
    )

    @pl.when(step == pl.num_programs(0) - 1)
    def _():
        direction = 2 * core - 1
        groups = half // LANES

        def store(pieces, stats):
            copies = []
            for b in range(count):
                part = slice(groups * b, groups * b + groups)
                write((kept.at[b], sent.at[b]), pieces[part], [kind[part] for kind in stats], core)
                move = {"own": 0, "near": direction, "back": -direction, "far": 2}[which[b]]
                block = lax.rem(z + SIDE + move, SIDE)
                copies.append(pltpu.make_async_copy(kept.at[b], kept_out.at[:, block], sem.at[2 * b]))
                copies.append(pltpu.make_async_copy(sent.at[b], sent_out.at[:, block], sem.at[2 * b + 1]))
            for copy in copies:
                copy.start()
            for copy in copies:
                copy.wait()

        summarise(logits[:columns, :], table_ref[...], core, store)


def message_rows(half):
    return (OWN + KINDS) * (half // LANES)


def whole_blocks(weights, table, which, buffers, previous):
    columns, depth = weights.shape
    features, half = buffers[0].shape[2:]
    count = len(which)
    width = half * count
    rows = message_rows(half)
    steps = pl.cdiv(columns, ROW_BLOCK)
    shape = jax.ShapeDtypeStruct((PLANE, SIDE, rows, LANES), jnp.float32)
    return pl.pallas_call(
        functools.partial(whole_kernel, which=which),
        grid=(steps,),
        in_specs=[pl.BlockSpec((ROW_BLOCK, depth), lambda i: (i, 0)), pl.BlockSpec(table.shape, lambda i: (0, 0))]
        + [ANY] * (2 * count + len(previous)),
        out_specs=[ANY, ANY],
        out_shape=[shape, shape],
        input_output_aliases={2 + 2 * count + k: k for k in range(len(previous))},
        scratch_shapes=[
            pltpu.VMEM((SIDE, SIDE, CORES, features, width), jnp.bfloat16),
            pltpu.VMEM((steps * ROW_BLOCK, width), jnp.float32),
            pltpu.VMEM((count, PLANE, rows, LANES), jnp.float32),
            pltpu.VMEM((count, PLANE, rows, LANES), jnp.float32),
            pltpu.SemaphoreType.DMA((2 * count,)),
        ],
        compiler_params=pltpu.CompilerParams(vmem_limit_bytes=VMEM_BYTES),
        cost_estimate=pl.CostEstimate(
            flops=2 * columns * (depth + B) * width,
            bytes_accessed=2 * depth * (columns + width),
            transcendentals=columns * width,
        ),
    )(weights, table, *buffers, *previous)


def finish_kernel(w_hbm, table_ref, *refs):
    part_b, outs, refs = refs[:8], refs[8:10], refs[10:]
    weights, held, logits, kept, sent, w_sem, x_sem, out_sem = refs
    step = pl.program_id(0)
    (x, _, _), core = position()
    columns = table_ref.shape[1]
    half = held.shape[5] // 2
    groups = half // LANES
    depth = weights.shape[1]
    direction = 2 * core - 1

    def w_copy(k):
        rows = pl.ds(ROW_BLOCK * k, min(ROW_BLOCK, columns - ROW_BLOCK * k))
        return pltpu.make_async_copy(w_hbm.at[rows], weights.at[rows], w_sem.at[k])

    def fetch_b(pair, slot):
        for k in range(8):
            move = (0, 0, direction, direction, -direction, -direction, 2, 2)[k]
            c = core if k in (0, 2, 5, 6) else 1 - core
            for h in range(2):
                target = held.at[slot, lax.rem(x + SIDE + move, SIDE), :, c, :, pl.ds(half * h, half)]
                pltpu.make_async_copy(part_b[k].at[2 * pair + h], target, x_sem.at[slot]).start()

    def arrived(slot, lanes):
        target = held.at[slot, :, :, :, :, pl.ds(0, lanes)]
        pltpu.make_async_copy(target, target, x_sem.at[slot]).wait()

    def send(b, outs, block):
        for k, source in enumerate((kept, sent)):
            pltpu.make_async_copy(source.at[b], outs[k].at[:, block], out_sem.at[b, k]).start()

    def store(pieces, stats):
        for h in range(2):
            part = slice(groups * h, groups * h + groups)
            b = 2 * step + h
            write((kept.at[b], sent.at[b]), pieces[part], [kind[part] for kind in stats], core)
            send(b, outs, b)

    @pl.when(step == 0)
    def _():
        w_copy(0).start()
        fetch_b(0, 0)
        for k in range(1, w_sem.shape[0]):
            w_copy(k).start()
        fetch_b(1, 1)
        arrived(0, 2 * half)
        tokens = held[0].reshape(depth, 2 * half)
        for k in range(w_sem.shape[0]):
            w_copy(k).wait()
            rows = slice(ROW_BLOCK * k, min(columns, ROW_BLOCK * (k + 1)))
            logits[rows, :] = jnp.dot(weights[rows, :], tokens, preferred_element_type=jnp.float32)
        summarise(logits[...], table_ref[...], core, store)

    @pl.when(step > 0)
    def _():
        arrived(1, 2 * half)
        tokens = held[1].reshape(depth, 2 * half)
        product = jnp.dot(weights[...], tokens, preferred_element_type=jnp.float32)
        summarise(product, table_ref[...], core, store)

    @pl.when(step == pl.num_programs(0) - 1)
    def _():
        for b in range(SIDE):
            for k, source in enumerate((kept, sent)):
                pltpu.make_async_copy(source.at[b], source.at[b], out_sem.at[b, k]).wait()


def finish(weights, table, part_b):
    columns, depth = weights.shape
    features, half = part_b[0].shape[2:]
    rows = message_rows(half)
    shape = jax.ShapeDtypeStruct((PLANE, SIDE, rows, LANES), jnp.float32)
    return pl.pallas_call(
        finish_kernel,
        grid=(2,),
        in_specs=[ANY, pl.BlockSpec(table.shape, lambda i: (0, 0))] + [ANY] * 8,
        out_specs=[ANY] * 2,
        out_shape=[shape] * 2,
        scratch_shapes=[
            pltpu.VMEM((columns, depth), jnp.bfloat16),
            pltpu.VMEM((2, SIDE, SIDE, CORES, features, 2 * half), jnp.bfloat16),
            pltpu.VMEM((columns, 2 * half), jnp.float32),
            pltpu.VMEM((SIDE, PLANE, rows, LANES), jnp.float32),
            pltpu.VMEM((SIDE, PLANE, rows, LANES), jnp.float32),
            pltpu.SemaphoreType.DMA((pl.cdiv(columns, ROW_BLOCK),)),
            pltpu.SemaphoreType.DMA((2,)),
            pltpu.SemaphoreType.DMA((SIDE, 2)),
        ],
        compiler_params=pltpu.CompilerParams(vmem_limit_bytes=VMEM_BYTES),
        cost_estimate=pl.CostEstimate(
            flops=2 * columns * (depth + B) * SIDE * half,
            bytes_accessed=2 * depth * (columns + SIDE * half),
            transcendentals=columns * SIDE * half,
        ),
    )(weights, table, *part_b)


def unpack(message, groups):
    lead = message.shape[:-2]
    sums = message[..., : OWN * groups, :].reshape(*lead, groups, OWN, LANES)
    stats = message[..., OWN * groups :, :].reshape(*lead, KINDS, groups, LANES)
    return sums, [stats[..., k, :, :] for k in range(KINDS)]


def merge(kept, received, groups):
    sums_a, (max_a, total_a, *_) = unpack(kept, groups)
    sums_b, (max_b, total_b, *_) = unpack(received, groups)
    local_max = jnp.maximum(max_a, max_b)
    scale_a = jnp.exp(max_a - local_max)
    scale_b = jnp.exp(max_b - local_max)
    sums = sums_a * scale_a[..., None, :] + sums_b * scale_b[..., None, :]
    excess = total_a * scale_a + total_b * scale_b - 1.0
    high = lax.reduce_precision(local_max, 8, 7)
    middle = lax.reduce_precision(local_max - high, 8, 7)
    low = local_max - high - middle
    return [sums.reshape(*kept.shape[:-2], OWN * groups, LANES), high, middle, low, excess]


def per_device(hidden_states, head_weight, sign_bits, bucket_ids):
    width, features = hidden_states.shape
    half = width // 2
    groups = half // LANES
    weights = head_weight.T
    columns = weights.shape[0]
    buckets = lax.broadcasted_iota(jnp.int32, (B, columns), 0)
    table = jnp.where(buckets == bucket_ids[None, :], 2 * sign_bits[None, :] - 1, 0).astype(jnp.bfloat16)

    part_a, part_b = place(place_first_kernel, around(hidden_states.T, Y), (SIDE, features, half))
    own = place(place_second_kernel, around_by_ring(part_a, X) + around_by_ring(part_b, Z), (SIDE, SIDE, features, half))
    near = [ring(p, a) for p, a in zip(own, (Z, X))]
    other = [swap(p) for p in own]
    message_a = whole_blocks(weights, table, ("own",), (own[0], other[0]), ())
    other, message_a = lax.optimization_barrier((other, message_a))
    near_other = [ring(p, a) for p, a in zip(other, (Z, X))]
    near = lax.optimization_barrier(near)
    far = [ring(p, a) for p, a in zip(near, (Z, X))]
    back = [swap(p) for p in near]
    back_other = [swap(p) for p in near_other]
    message_a = whole_blocks(weights, table, ("near", "back"), (near[0], near_other[0], back[0], back_other[0]), message_a)
    far, back, back_other, message_a = lax.optimization_barrier((far, back, back_other, message_a))
    far_other = [swap(p) for p in far]
    part_b = (own[1], other[1], near[1], near_other[1], back[1], back_other[1], far[1], far_other[1])
    message_a = whole_blocks(weights, table, ("far",), (far[0], far_other[0]), message_a)
    message_b = finish(weights, table, part_b)

    pieces = []
    for kept, sent in (message_a, message_b):
        pieces += merge(kept, swap(sent), groups)
    packed = jnp.concatenate(pieces, axis=2).astype(jnp.float16)
    teams = [[device_at(x, y, z, c) for x in range(SIDE) for y in range(SIDE) for z in range(SIDE)] for c in range(CORES)]
    packed = packed.reshape(PLANE * SIDE, packed.shape[2], LANES)
    received = lax.all_to_all(packed, BOTH, 0, 0, axis_index_groups=teams, tiled=True).astype(jnp.float32)
    sums, (high, middle, low, excess) = unpack(received.reshape(PLANE * SIDE, 2, -1, LANES), groups)
    local_max = high + middle + low
    rescale = jnp.exp(local_max - jnp.max(local_max, axis=0))
    row_total = jnp.sum((1.0 + excess) * rescale, axis=0)
    bucket_sums = jnp.sum(sums * rescale[..., None, :], axis=0)
    factor = jnp.sqrt(jnp.float32(V) * jnp.float32(B))
    sketch = bucket_sums / row_total[..., None, :] * factor
    return (sketch.transpose(0, 1, 3, 2).reshape(width, OWN), -jnp.log(row_total).reshape(width))


def solution(mesh):
    return jax.shard_map(
        per_device,
        mesh=mesh,
        in_specs=(
            P("rows", "vocab"),
            P(None, ("vocab", "rows")),
            P(("vocab", "rows")),
            P(("vocab", "rows")),
        ),
        out_specs=(P("rows", "vocab"), P("rows")),
        check_vma=False,
    )
```
